32 devices in a mesh: groups: 2 (over x), region: 16 (over z, y, core).
Axes of the slice: x: 2, y: 2, z: 4, core: 2. Of those that a mesh axis runs over, the one named last changes fastest.
Arguments:
- environment: bfloat16 [160, 96, 3264], P(('groups', 'region')), parts along dimension 0, may hold values from -6 to 6
- site_tensors: bfloat16 [160, 1, 4, 96, 96], P(('groups', 'region')), parts along dimension 0, may hold values from -0.625 to 0.625
- operator_blocks: bfloat16 [34, 4, 34], replicated, may hold values from -0.5 to 0.5
- join_in: int32 [80, 4], P('groups'), parts along dimension 0, may hold values from -1 to 39, as said below
- block_sizes: int32 [80], P('groups'), parts along dimension 0, may hold values from 48 to 96
Outputs:
- advanced: bfloat16 [160, 96, 3264], P(('groups', 'region')), parts along dimension 0
The draws below stay inside these ranges and needn't reach their ends.
There are 2 independent parts, one for each index of `groups`. The reference program is written for one: setup_inputs(seed, part) draws one part's arguments, and reference() takes and returns one part's arrays. A program takes and returns all parts, laid end to end along the dimension named above; an argument that names none is the same for every part. Nothing has to cross between parts.
Inputs may be any that keep to these rules, and one draw needn't show every extreme that they name: Sectors are ordered by particle number, then spin, with at most 5 sectors to one particle number; a site adds 0 to 2 particles, so join_in[b, 0] = b and every other entry is -1 or lies between b - 2 * 5 + 1 and b - 1.
All inputs are finite; a program needn't handle non-finite values.
Results may differ from the reference program's by a relative error of at most 0.0058.
Values may be sent and summed in bfloat16 or wider, within the bound.
No kernel may reach another device: no remote copies, remote signals or barrier semaphores. Data moves between devices by JAX's collectives and lax.ppermute only.
A program may use at most 128 MiB of HBM per device.

```python
import jax
import jax.numpy as jnp
from jax import lax

NSEC = 40
TILE = 96
CH = 34
PHYS = 4
OWN = 8
ITERS = 1
NREG = 2


def draw_join_in(key, part):
    key = jax.random.fold_in(key, 11)
    first_key, second_key = jax.random.split(key)
    reach = 2 * (NSEC // OWN) - 1
    sectors = jnp.arange(NSEC, dtype=jnp.int32)
    offsets = jax.random.randint(first_key, (NSEC, PHYS - 1), 1, reach + 1)
    present = jax.random.randint(second_key, (NSEC, PHYS - 1), 0, 4) > 0
    offsets = offsets.at[NSEC - 1, PHYS - 2].set(reach)
    present = present.at[NSEC - 1, PHYS - 2].set(True)
    lower = sectors[:, None] - offsets
    lower = jnp.where(present & (lower >= 0), lower, -1)
    return jnp.concatenate([sectors[:, None], lower], axis=1).astype(jnp.int32)


def draw_block_sizes(key, part):
    key = jax.random.fold_in(key, 23)
    first_key, second_key = jax.random.split(key)
    sizes = TILE - jax.random.randint(first_key, (NSEC,), 0, TILE // 2 + 1)
    fullest = jax.random.randint(second_key, (), 0, NSEC)
    return jnp.where(jnp.arange(NSEC) == fullest, TILE, sizes).astype(jnp.int32)


def levels(key, shape, cuts, low, largest):
    level = 1.0
    for dim, parts in cuts:
        heights = jax.random.uniform(jax.random.fold_in(jax.random.fold_in(key, 6), dim), (parts,), jnp.float32, low / len(cuts), largest / len(cuts))
        level = level * jnp.repeat(jnp.exp(heights), shape[dim] // parts).reshape((-1,) + (1,) * (len(shape) - 1 - dim))
    return level


def scatter_about(stream_key, extent, deviation, most, shards=(), held_as=jnp.bfloat16):
    array = deviation * jax.random.normal(stream_key, extent, jnp.float32)
    if shards:
        array = array * levels(stream_key, extent, shards, -0.22, 0.18)
    return jnp.clip(array, -most, most).astype(held_as)


def setup_inputs(seed: int = 0, part: int = 0) -> dict:
    splits = jax.random.split(jax.random.key(seed), 6)
    own_keys = jax.random.split(jax.random.fold_in(splits[5], part), 6)
    return {
        "environment": scatter_about(own_keys[0], (NREG * NSEC, TILE, CH * TILE), 1.0, 6.0, ((0, 16),)),
        "site_tensors": scatter_about(own_keys[1], (NREG * NSEC, ITERS, PHYS, TILE, TILE), TILE ** -0.5, 0.625, ((0, 16),)),
        "operator_blocks": scatter_about(splits[2], (CH, PHYS, CH), (PHYS * CH) ** -0.5, 0.5),
        "join_in": draw_join_in(jax.random.fold_in(jax.random.fold_in(splits[5], part), 71), part),
        "block_sizes": draw_block_sizes(jax.random.fold_in(jax.random.fold_in(splits[5], part), 71), part),
    }


def advance_region(current, tensors, operator_blocks, join_in, block_sizes):
    valid = join_in >= 0
    source = jnp.where(valid, join_in, 0)
    sizes_in = block_sizes[source]
    rows = jnp.arange(TILE, dtype=jnp.int32)
    keep = valid[:, :, None, None] & (rows[None, None, :, None] < sizes_in[:, :, None, None]) & (rows[None, None, None, :] < block_sizes[:, None, None, None])
    masked = jnp.where(keep, tensors, jnp.zeros_like(tensors))
    pieces = []
    for state_index in range(PHYS):
        blocks = current[source[:, state_index]].astype(jnp.float32)
        left = jnp.einsum('bxu,bxz->buz', masked[:, state_index].astype(jnp.float32), blocks)
        left = lax.optimization_barrier(left.astype(jnp.bfloat16)).astype(jnp.float32)
        left = left.reshape(NSEC, TILE, CH, TILE)
        mixed = jnp.einsum('buwy,wk->buky', left, operator_blocks[:, state_index, :].astype(jnp.float32))
        mixed = lax.optimization_barrier(mixed.astype(jnp.bfloat16)).astype(jnp.float32)
        pieces.append(mixed)
    stacked = jnp.stack(pieces, axis=1)
    result = jnp.einsum('bpuky,bpyv->bukv', stacked, masked.astype(jnp.float32))
    return result.astype(jnp.bfloat16).reshape(NSEC, TILE, CH * TILE)


def reference(environment, site_tensors, operator_blocks, join_in, block_sizes):
    regions = environment.reshape(NREG, NSEC, TILE, CH * TILE)
    current = jnp.roll(regions, 1, axis=0)
    tensors = site_tensors.reshape(NREG, NSEC, ITERS, PHYS, TILE, TILE)
    for section in range(ITERS):
        current = lax.map(lambda pair: advance_region(pair[0], pair[1], operator_blocks, join_in, block_sizes), (current, tensors[:, :, section]))
    return current.reshape(NREG * NSEC, TILE, CH * TILE)
```

```python
import functools

import jax
import jax.numpy as jnp
from jax import lax
from jax.experimental import pallas as pl
from jax.experimental.pallas import tpu as pltpu
from jax.sharding import PartitionSpec as P

OWN = 8
LANES = 128
ROWS = 40
GROUP = 6


def shifted(value, axis, steps):
    count = lax.axis_size(axis)
    return lax.ppermute(value, axis, [(source, (source + steps) % count) for source in range(count)])


def to_next(value, axis, first):
    count = lax.axis_size(axis)
    pairs = [(source, source + 1) for source in range(count) if first <= source % OWN < OWN - 1]
    return lax.ppermute(value, axis, pairs)


def stage_kernel(first, last, blocks, offs, *refs):
    block_refs = refs[:blocks]
    gt_ref, gy_ref, mix_ref = refs[blocks : blocks + 3]
    acc_in = None if first else refs[blocks + 3]
    result, slab, yf, *rest = refs[blocks + 3 + (not first) :]
    tile = gt_ref.shape[-1]
    states = mix_ref.shape[0]
    chans = block_refs[0].shape[-1] // tile
    span = GROUP * ROWS
    b = pl.program_id(0)
    acc = rest[0] if last else result.at[0]

    @pl.when(b == 0)
    def _():
        yf[...] = jnp.zeros_like(yf)
        pad = jnp.zeros((tile, LANES - tile), jnp.bfloat16)
        place = 0
        for ref in block_refs:
            for i in range(ref.shape[0]):
                for w in range(chans):
                    piece = ref[i, :, w * tile : (w + 1) * tile]
                    slab[place, :, w * LANES : (w + 1) * LANES] = jnp.concatenate([piece, pad], axis=1)
                place += 1

    acc[...] = jnp.zeros(acc.shape, jnp.float32) if first else acc_in[0]
    for q in range(states):
        a = offs[b, q]

        @pl.when(a >= 0)
        def _():
            for c in range(0, chans, 2):
                y = jnp.dot(gt_ref[0, q], slab[a, :, c * LANES : (c + 2) * LANES], preferred_element_type=jnp.float32)
                yf[pl.ds(c, tile, stride=ROWS), :] = y[:, :LANES]
                yf[pl.ds(c + 1, tile, stride=ROWS), :] = y[:, LANES:]
            for g in range(0, tile // GROUP, 2):
                one, two = (slice((g + k) * span, (g + k + 1) * span) for k in range(2))
                rhs = jnp.concatenate([yf[one, :].astype(jnp.bfloat16), yf[two, :].astype(jnp.bfloat16)], axis=1)
                v = jnp.dot(mix_ref[q], rhs, preferred_element_type=jnp.float32).astype(jnp.bfloat16)
                acc[one, :] += jnp.dot(v[:, :LANES], gy_ref[0, q], preferred_element_type=jnp.float32)
                acc[two, :] += jnp.dot(v[:, LANES:], gy_ref[0, q], preferred_element_type=jnp.float32)

    if last:
        for w in range(chans):
            done = acc[pl.ds(w, tile, stride=ROWS), :].astype(jnp.bfloat16)
            result[0, :, w * tile : (w + 1) * tile] = done[:, :tile]


def stage(offs, arrays, gt, gy, mix, acc, last, chans):
    slots, states, tile, _ = gt.shape
    first = acc is None
    total = sum(a.shape[0] for a in arrays)
    full = tile * ROWS

    def whole(a):
        return pl.BlockSpec(a.shape, lambda b, offs: (0,) * a.ndim)

    def one(a):
        return pl.BlockSpec((1,) + a.shape[1:], lambda b, offs: (b,) + (0,) * (a.ndim - 1))

    args = list(arrays) + [gt, gy, mix]
    specs = [whole(a) for a in arrays] + [one(gt), one(gy), whole(mix)]
    if not first:
        args.append(acc)
        specs.append(one(acc))
    if last:
        out = jax.ShapeDtypeStruct((slots, tile, chans * tile), jnp.bfloat16)
    else:
        out = jax.ShapeDtypeStruct((slots, full, LANES), jnp.float32)
    scratch = [pltpu.VMEM((total, tile, chans * LANES), jnp.bfloat16), pltpu.VMEM((full, LANES), jnp.float32)]
    if last:
        scratch.append(pltpu.VMEM((full, LANES), jnp.float32))
    aliases = {} if first or last else {len(args): 0}
    flops = 2 * slots * states * tile * tile * chans * (2 * tile + chans) * total // (3 * slots)
    return pl.pallas_call(
        functools.partial(stage_kernel, first, last, len(arrays)),
        out_shape=out,
        grid_spec=pltpu.PrefetchScalarGridSpec(
            num_scalar_prefetch=1, grid=(slots,), in_specs=specs, out_specs=one(out), scratch_shapes=scratch
        ),
        input_output_aliases=aliases,
        compiler_params=pltpu.CompilerParams(vmem_limit_bytes=40 * 1024 * 1024),
        cost_estimate=pl.CostEstimate(flops=flops * 8, bytes_accessed=8 * 1024 * 1024, transcendentals=0),
    )(offs, *args)


def tied(value, after):
    return lax.optimization_barrier((value, after))[0]


def per_device(environment, site_tensors, operator_blocks, join_in, block_sizes):
    slots, tile, _ = environment.shape
    chans, states, _ = operator_blocks.shape
    base = (lax.axis_index("region") % OWN) * slots

    order = list(reversed(range(slots)))
    received = {}
    for place, slot in enumerate(order):
        block = environment[slot : slot + 1]
        if place >= 2:
            block = tied(block, received[order[place - 2]])
        received[slot] = shifted(block, "region", OWN)

    tensors = site_tensors[:, 0]
    own_rows = lax.dynamic_slice_in_dim(join_in, base, slots, 0)
    own_sizes = lax.dynamic_slice_in_dim(block_sizes, base, slots, 0)
    valid = own_rows >= 0
    sizes_in = jnp.take(block_sizes, jnp.where(valid, own_rows, 0), axis=0)
    rows = jnp.arange(tile, dtype=jnp.int32)
    keep = (
        valid[:, :, None, None]
        & (rows[None, None, :, None] < sizes_in[:, :, None, None])
        & (rows[None, None, None, :] < own_sizes[:, None, None, None])
    )
    masked = jnp.where(keep, tensors, jnp.zeros_like(tensors))
    gt = jnp.swapaxes(masked, 2, 3)
    gy = jnp.pad(masked, ((0, 0), (0, 0), (0, LANES - tile), (0, LANES - tile)))
    ops = jnp.pad(jnp.transpose(operator_blocks, (1, 2, 0)), ((0, 0), (0, ROWS - chans), (0, ROWS - chans)))
    mix = jnp.einsum("gh,qkw->qgkhw", jnp.eye(GROUP, dtype=ops.dtype), ops)
    mix = mix.reshape(states, GROUP * ROWS, GROUP * ROWS)

    place = own_rows - base + 2 * slots
    hop = 2 - place // slots
    slot_of = place % slots
    groups = [order[i : i + 2] for i in range(0, slots, 2)]
    acc = None
    for number, group in enumerate(groups):
        last = number == len(groups) - 1
        here = jnp.concatenate([received[slot] for slot in group], axis=0)
        one = to_next(here, "region", 0)
        arrays = [here, one]
        if group != [0]:
            arrays.append(to_next(one, "region", 1))
        count = len(group)
        index = group[0] - slot_of
        mine = valid & (index >= 0) & (index < count)
        offs = jnp.where(mine, hop * count + index, -1).astype(jnp.int32)
        acc = stage(offs, arrays, gt, gy, mix, acc, last, chans)
    return acc


def solution(mesh):
    placed = (
        P(("groups", "region"), None, None),
        P(("groups", "region"), None, None, None, None),
        P(),
        P("groups", None),
        P("groups"),
    )
    return jax.shard_map(
        per_device,
        mesh=mesh,
        in_specs=placed,
        out_specs=P(("groups", "region"), None, None),
        check_vma=False,
    )
```

```python
import functools

import jax
import jax.numpy as jnp
from jax import lax
from jax.experimental import pallas as pl
from jax.experimental.pallas import tpu as pltpu
from jax.sharding import PartitionSpec as P

OWN = 8
LANES = 128
CHUNK = 544
STEP = 16
GROUP = 4


def shifted(value, axis, steps):
    count = lax.axis_size(axis)
    return lax.ppermute(value, axis, [(source, (source + steps) % count) for source in range(count)])


def to_next(value, axis):
    count = lax.axis_size(axis)
    pairs = [(source, source + 1) for source in range(count) if source % OWN < OWN - 1]
    return lax.ppermute(value, axis, pairs)


def to_second(value, from_last, axis):
    count = lax.axis_size(axis)
    middle = OWN // 2
    regions = range(0, count, OWN)
    relay = lax.ppermute(value, axis, [(r + middle - 2, r) for r in regions])
    steps = [(0, middle)] + [(o, o + 1) for o in range(1, OWN - 1) if o != middle - 1]
    sent = jnp.where(lax.axis_index(axis) % OWN == 0, relay, from_last)
    return lax.ppermute(sent, axis, [(r + a, r + b) for r in regions for a, b in steps])


def tied(value, *after):
    return lax.optimization_barrier((value, after))[0]


def more_units(size, low, tile):
    units = (size > low).astype(jnp.int32)
    for start in range(low + STEP, tile, STEP):
        units += (size > start).astype(jnp.int32)
    return units


def base_copies(parts, low, env_ref, base_refs, sems):
    copies = []
    for number, (part, ref) in enumerate(zip(parts, base_refs)):
        source = env_ref.at[part.start : part.stop, :low]
        copies.append(pltpu.make_async_copy(source, ref, sems.at[number]))
    for copy in copies:
        copy.start()
    return copies


def pool_kernel(slots, parts, low, tile, owner, sizes, env_ref, rest_ref, *refs):
    *base_refs, out_ref, sems = refs
    copies = base_copies(parts, low, env_ref, base_refs, sems)
    at = jnp.int32(0)
    for slot in reversed(range(slots)):
        units = more_units(sizes[owner[0] * slots + slot], low, tile)
        for unit in range((tile - low) // STEP):

            @pl.when(unit < units)
            def _():
                out_ref[at + unit] = rest_ref[slot, unit * STEP : (unit + 1) * STEP, :]

        at += units
    for copy in copies:
        copy.wait()


def pooled(owner, sizes, environment, parts, low):
    slots, tile, wide = environment.shape
    rest = tile - low
    outs = [jax.ShapeDtypeStruct((len(part), low, wide), environment.dtype) for part in parts]
    pool = jax.ShapeDtypeStruct((slots * rest // STEP, STEP, wide), environment.dtype)
    *bases, pool = pl.pallas_call(
        functools.partial(pool_kernel, slots, parts, low, tile),
        out_shape=outs + [pool],
        grid_spec=pltpu.PrefetchScalarGridSpec(
            num_scalar_prefetch=2,
            grid=(1,),
            in_specs=[
                pl.BlockSpec(memory_space=pl.ANY),
                pl.BlockSpec((slots, rest, wide), lambda i, *_: (0, low // rest, 0)),
            ],
            out_specs=[pl.BlockSpec(memory_space=pl.ANY)] * len(parts)
            + [pl.BlockSpec(pool.shape, lambda i, *_: (0, 0, 0))],
            scratch_shapes=[pltpu.SemaphoreType.DMA((len(parts),))],
        ),
        compiler_params=pltpu.CompilerParams(vmem_limit_bytes=8 * 1024 * 1024),
        cost_estimate=pl.CostEstimate(flops=1000, bytes_accessed=1024, transcendentals=0),
    )(owner, sizes, environment, environment)
    return bases, pool


def pool_shifted(total, pool):
    def branch(units):
        def run(value):
            if units == 0:
                return value
            if units == value.shape[0]:
                return shifted(value, "region", OWN)
            return lax.dynamic_update_slice(value, shifted(value[:units], "region", OWN), (0, 0, 0))

        return run

    return lax.switch(total, [branch(units) for units in range(pool.shape[0] + 1)], pool)


def stage_kernel(first, last, wanted, hops, slots, owner, join, sizes, *refs):
    count = len(wanted)
    listed = [(hop, part[i], ref, i) for ref, (hop, part) in enumerate(wanted) for i in range(len(part))]
    block_refs, refs = refs[:count], refs[count:]
    pool_refs, refs = refs[:hops], refs[hops:]
    count = 0
    site_ref, ops_ref = refs[count : count + 2]
    acc_in = None if first else refs[count + 2]
    result, slab, mix, yf, vb, *rest = refs[count + 2 + (not first) :]
    tile = site_ref.shape[-1]
    states = ops_ref.shape[0]
    chans = block_refs[0].shape[-1] // tile
    span = GROUP * chans
    b = pl.program_id(0)
    base = owner[0] * slots
    acc = rest[0] if last else result.at[0]

    @pl.when(b == 0)
    def _():
        low = block_refs[0].shape[1]

        def spread(place, rows, value):
            pad = jnp.zeros((rows.stop - rows.start, LANES - tile), jnp.bfloat16)
            for w in range(chans):
                piece = value[:, w * tile : (w + 1) * tile]
                slab[place, rows, w * LANES : (w + 1) * LANES] = jnp.concatenate([piece, pad], axis=1)

        for place, (hop, slot, ref, index) in enumerate(listed):
            spread(place, slice(0, low), block_refs[ref][index])
            holder = jnp.maximum(owner[0] - hop, 0) * slots
            at = jnp.int32(0)
            for other in range(slot + 1, slots):
                at += more_units(sizes[holder + other], low, tile)
            units = more_units(sizes[holder + slot], low, tile)
            for unit in range((tile - low) // STEP):
                rows = slice(low + unit * STEP, low + (unit + 1) * STEP)

                @pl.when(unit < units)
                def _():
                    spread(place, rows, pool_refs[hop][at + unit])

                @pl.when(unit >= units)
                def _():
                    slab[place, rows, :] = jnp.zeros((STEP, chans * LANES), jnp.bfloat16)

        row = lax.broadcasted_iota(jnp.int32, (span, chans), 0)
        channel = lax.broadcasted_iota(jnp.int32, (span, chans), 1)
        pick = jnp.zeros((span, chans), jnp.bfloat16)
        for g in range(GROUP):
            pick += (row == channel + g * chans).astype(jnp.float32).astype(jnp.bfloat16)
        left = lax.broadcasted_iota(jnp.int32, (span, span), 0)
        right = lax.broadcasted_iota(jnp.int32, (span, span), 1)
        same = jnp.zeros((span, span), jnp.bool_)
        for g in range(GROUP):
            low_end, high_end = g * chans, (g + 1) * chans
            same |= (left >= low_end) & (left < high_end) & (right >= low_end) & (right < high_end)
        for q in range(states):
            spread_rows = jnp.dot(pick, ops_ref[q], preferred_element_type=jnp.float32).astype(jnp.bfloat16)
            both = lax.dot_general(spread_rows, pick, (((1,), (1,)), ((), ())), preferred_element_type=jnp.float32)
            mix[q] = jnp.where(same, both, 0.0).astype(jnp.bfloat16)

    acc[...] = jnp.zeros(acc.shape, jnp.float32) if first else acc_in[0]
    own_size = sizes[base + b]
    for q in range(states):
        a = join[base + b, q]
        place = jnp.int32(-1)
        for at, (hop, slot, _, _) in enumerate(listed):
            place = jnp.where(a - base == slot - hop * slots, at, place)

        @pl.when((a >= 0) & (place >= 0))
        def _():
            x = lax.broadcasted_iota(jnp.int32, (tile, tile), 0)
            u = lax.broadcasted_iota(jnp.int32, (tile, tile), 1)
            keep = (x < sizes[jnp.maximum(a, 0)]) & (u < own_size)
            g32 = jnp.where(keep, site_ref[0, 0, q].astype(jnp.float32), 0.0)
            gt = g32.T.astype(jnp.bfloat16)
            gy = jnp.concatenate([g32, jnp.zeros((tile, LANES - tile), jnp.float32)], axis=1)
            gy = jnp.concatenate([gy, jnp.zeros((LANES - tile, LANES), jnp.float32)], axis=0).astype(jnp.bfloat16)
            for c in range(0, chans, 2):
                y = jnp.dot(gt, slab[place, :, c * LANES : (c + 2) * LANES], preferred_element_type=jnp.float32)
                yf[pl.ds(c, tile, stride=chans), :] = y[:, :LANES]
                yf[pl.ds(c + 1, tile, stride=chans), :] = y[:, LANES:]
            for g in range(0, tile // GROUP, 2):
                one, two = (slice((g + k) * span, (g + k + 1) * span) for k in range(2))
                rhs = jnp.concatenate([yf[one, :].astype(jnp.bfloat16), yf[two, :].astype(jnp.bfloat16)], axis=1)
                v = jnp.dot(mix[q], rhs, preferred_element_type=jnp.float32)
                v = jnp.concatenate([v[:, :LANES], v[:, LANES:]], axis=0).astype(jnp.bfloat16)
                vb[g * span : (g + 2) * span, :] = v
            for g in range(0, tile * chans, CHUNK):
                some = slice(g, g + CHUNK)
                acc[some, :] += jnp.dot(vb[some, :], gy, preferred_element_type=jnp.float32)

    if last:
        for w in range(chans):
            done = acc[pl.ds(w, tile, stride=chans), :].astype(jnp.bfloat16)
            result[0, :, w * tile : (w + 1) * tile] = done[:, :tile]


def stage(owner, join, sizes, wanted, blocks, pools, tensors, ops, acc, last):
    slots, _, states, tile, _ = tensors.shape
    wide = blocks[0].shape[-1]
    chans = wide // tile
    first = acc is None
    full = tile * chans

    def whole(a):
        return pl.BlockSpec(a.shape, lambda b, *_: (0,) * a.ndim, pipeline_mode=pl.Buffered(1))

    def one(a):
        return pl.BlockSpec((1,) + a.shape[1:], lambda b, *_: (b,) + (0,) * (a.ndim - 1))

    args = list(blocks) + list(pools) + [tensors, ops]
    specs = [whole(a) for a in blocks] + [whole(a) for a in pools] + [one(tensors), whole(ops)]
    if not first:
        args.append(acc)
        specs.append(one(acc))
    if last:
        out = jax.ShapeDtypeStruct((slots, tile, wide), jnp.bfloat16)
    else:
        out = jax.ShapeDtypeStruct((slots, full, LANES), jnp.float32)
    scratch = [
        pltpu.VMEM((sum(len(part) for _, part in wanted), tile, chans * LANES), jnp.bfloat16),
        pltpu.VMEM((states, GROUP * chans, GROUP * chans), jnp.bfloat16),
        pltpu.VMEM((full, LANES), jnp.float32),
        pltpu.VMEM((full, LANES), jnp.bfloat16),
    ]
    if last:
        scratch.append(pltpu.VMEM((full, LANES), jnp.float32))
    aliases = {} if first or last else {len(args) + 2: 0}
    return pl.pallas_call(
        functools.partial(stage_kernel, first, last, tuple(wanted), len(pools), slots),
        out_shape=out,
        grid_spec=pltpu.PrefetchScalarGridSpec(
            num_scalar_prefetch=3, grid=(slots,), in_specs=specs, out_specs=one(out), scratch_shapes=scratch
        ),
        input_output_aliases=aliases,
        compiler_params=pltpu.CompilerParams(vmem_limit_bytes=48 * 1024 * 1024),
        cost_estimate=pl.CostEstimate(flops=10**10, bytes_accessed=2**20, transcendentals=0),
    )(owner, join, sizes, *args)


def per_device(environment, site_tensors, operator_blocks, join_in, block_sizes):
    slots, tile, _ = environment.shape
    chans = operator_blocks.shape[0]
    owner = (lax.axis_index("region") % OWN).astype(jnp.int32)
    low = tile * 2 // 3
    own_sizes = lax.dynamic_slice_in_dim(block_sizes, owner * slots, slots, 0)
    total = jnp.sum(more_units(own_sizes, low, tile))
    ops = jnp.transpose(operator_blocks, (1, 2, 0))
    owner = owner[None]

    parts = [range(max(0, stop - 2), stop) for stop in range(slots, 1, -2)] + [range(0, 1)]
    bases, pool = pooled(owner, block_sizes, environment, parts, low)
    pool = pool_shifted(total, pool)
    here, one, two = [], [], []
    for i in range(len(parts)):
        here.append(shifted(tied(bases[i], here[i - 1] if i else pool), "region", OWN))
    pool_one = to_next(pool, "region")
    kept = pool.shape[0] // slots * (slots - 1)
    pool_two = to_second(pool[:kept], pool_one[:kept], "region")
    pools = [pool, pool_one, pool_two]
    for i in range(len(parts)):
        one.append(to_next(here[i], "region"))
        if i + 1 < len(parts):
            two.append(to_second(here[i], one[i], "region"))

    late = len(parts) - 2
    early = [(hop, i) for i in range(late) for hop in range(3)] + [(0, late)]
    rest = [(1, late), (2, late), (0, late + 1), (1, late + 1)]
    acc = None
    for chosen in (early, rest):
        blocks = [(here, one, two)[hop][i] for hop, i in chosen]
        wanted = [(hop, parts[i]) for hop, i in chosen]
        acc = stage(owner, join_in, block_sizes, wanted, blocks, pools, site_tensors, ops, acc, chosen is rest)
    return acc


def solution(mesh):
    placed = (
        P(("groups", "region"), None, None),
        P(("groups", "region"), None, None, None, None),
        P(),
        P("groups", None),
        P("groups"),
    )
    return jax.shard_map(
        per_device,
        mesh=mesh,
        in_specs=placed,
        out_specs=P(("groups", "region"), None, None),
        check_vma=False,
    )
```

```python
import functools

import jax
import jax.numpy as jnp
from jax import lax
from jax.experimental import pallas as pl
from jax.experimental.pallas import tpu as pltpu
from jax.sharding import PartitionSpec as P

OWN = 8
LANES = 128
CHUNK = 544
STEP = 16
GROUP = 4


def shifted(value, axis, steps):
    count = lax.axis_size(axis)
    return lax.ppermute(value, axis, [(source, (source + steps) % count) for source in range(count)])


def to_next(value, axis):
    count = lax.axis_size(axis)
    pairs = [(source, source + 1) for source in range(count) if source % OWN < OWN - 1]
    return lax.ppermute(value, axis, pairs)


def to_second(value, from_last, axis):
    count = lax.axis_size(axis)
    middle = OWN // 2
    regions = range(0, count, OWN)
    relay = lax.ppermute(value, axis, [(r + middle - 2, r) for r in regions])
    steps = [(0, middle)] + [(o, o + 1) for o in range(1, OWN - 1) if o != middle - 1]
    sent = jnp.where(lax.axis_index(axis) % OWN == 0, relay, from_last)
    return lax.ppermute(sent, axis, [(r + a, r + b) for r in regions for a, b in steps])


def tied(value, *after):
    return lax.optimization_barrier((value, after))[0]


def more_units(size, low, tile):
    units = (size > low).astype(jnp.int32)
    for start in range(low + STEP, tile, STEP):
        units += (size > start).astype(jnp.int32)
    return units


def base_copies(parts, low, env_ref, base_refs, sems):
    copies = []
    for number, (part, ref) in enumerate(zip(parts, base_refs)):
        source = env_ref.at[part.start : part.stop, :low]
        copies.append(pltpu.make_async_copy(source, ref, sems.at[number]))
    for copy in copies:
        copy.start()
    return copies


def pool_kernel(slots, parts, low, tile, owner, sizes, env_ref, *refs):
    *base_refs, out_ref, sems = refs
    copies = base_copies(parts, low, env_ref, base_refs, sems)
    at = jnp.int32(0)
    for slot in reversed(range(slots)):
        units = more_units(sizes[owner[0] * slots + slot], low, tile)
        for unit in range((tile - low) // STEP):

            @pl.when(unit < units)
            def _():
                out_ref[at + unit] = env_ref[slot, low + unit * STEP : low + (unit + 1) * STEP, :]

        at += units
    for copy in copies:
        copy.wait()


def pooled(owner, sizes, environment, parts, low):
    slots, tile, wide = environment.shape
    rest = tile - low
    outs = [jax.ShapeDtypeStruct((len(part), low, wide), environment.dtype) for part in parts]
    pool = jax.ShapeDtypeStruct((slots * rest // STEP, STEP, wide), environment.dtype)
    *bases, pool = pl.pallas_call(
        functools.partial(pool_kernel, slots, parts, low, tile),
        out_shape=outs + [pool],
        grid_spec=pltpu.PrefetchScalarGridSpec(
            num_scalar_prefetch=2,
            grid=(1,),
            in_specs=[pl.BlockSpec((slots, tile, wide), lambda i, *_: (0, 0, 0), pipeline_mode=pl.Buffered(1))],
            out_specs=[pl.BlockSpec(memory_space=pl.ANY)] * len(parts)
            + [pl.BlockSpec(pool.shape, lambda i, *_: (0, 0, 0))],
            scratch_shapes=[pltpu.SemaphoreType.DMA((len(parts),))],
        ),
        compiler_params=pltpu.CompilerParams(vmem_limit_bytes=60 * 1024 * 1024),
        cost_estimate=pl.CostEstimate(flops=1000, bytes_accessed=1024, transcendentals=0),
    )(owner, sizes, environment)
    return bases, pool


def pool_shifted(total, pool):
    def branch(units):
        def run(value):
            if units == 0:
                return value
            if units == value.shape[0]:
                return shifted(value, "region", OWN)
            return lax.dynamic_update_slice(value, shifted(value[:units], "region", OWN), (0, 0, 0))

        return run

    return lax.switch(total, [branch(units) for units in range(pool.shape[0] + 1)], pool)


def stage_kernel(first, last, wanted, hops, slots, owner, join, sizes, *refs):
    count = len(wanted)
    listed = [(hop, part[i], ref, i) for ref, (hop, part) in enumerate(wanted) for i in range(len(part))]
    block_refs, refs = refs[:count], refs[count:]
    pool_refs, refs = refs[:hops], refs[hops:]
    count = 0
    site_ref, ops_ref = refs[count : count + 2]
    acc_in = None if first else refs[count + 2]
    result, slab, mix, yf, vb, *rest = refs[count + 2 + (not first) :]
    tile = site_ref.shape[-1]
    states = ops_ref.shape[0]
    chans = block_refs[0].shape[-1] // tile
    span = GROUP * chans
    b = pl.program_id(0)
    base = owner[0] * slots
    acc = rest[0] if last else result.at[b]

    @pl.when(b == 0)
    def _():
        low = block_refs[0].shape[1]

        def spread(place, rows, value):
            pad = jnp.zeros((rows.stop - rows.start, LANES - tile), jnp.bfloat16)
            for w in range(chans):
                piece = value[:, w * tile : (w + 1) * tile]
                slab[place, rows, w * LANES : (w + 1) * LANES] = jnp.concatenate([piece, pad], axis=1)

        for place, (hop, slot, ref, index) in enumerate(listed):
            spread(place, slice(0, low), block_refs[ref][index])
            holder = jnp.maximum(owner[0] - hop, 0) * slots
            at = jnp.int32(0)
            for other in range(slot + 1, slots):
                at += more_units(sizes[holder + other], low, tile)
            units = more_units(sizes[holder + slot], low, tile)
            for unit in range((tile - low) // STEP):
                rows = slice(low + unit * STEP, low + (unit + 1) * STEP)

                @pl.when(unit < units)
                def _():
                    spread(place, rows, pool_refs[hop][at + unit])

                @pl.when(unit >= units)
                def _():
                    slab[place, rows, :] = jnp.zeros((STEP, chans * LANES), jnp.bfloat16)

        row = lax.broadcasted_iota(jnp.int32, (span, chans), 0)
        channel = lax.broadcasted_iota(jnp.int32, (span, chans), 1)
        pick = jnp.zeros((span, chans), jnp.bfloat16)
        for g in range(GROUP):
            pick += (row == channel + g * chans).astype(jnp.float32).astype(jnp.bfloat16)
        left = lax.broadcasted_iota(jnp.int32, (span, span), 0)
        right = lax.broadcasted_iota(jnp.int32, (span, span), 1)
        same = jnp.zeros((span, span), jnp.bool_)
        for g in range(GROUP):
            low_end, high_end = g * chans, (g + 1) * chans
            same |= (left >= low_end) & (left < high_end) & (right >= low_end) & (right < high_end)
        for q in range(states):
            spread_rows = jnp.dot(pick, ops_ref[q], preferred_element_type=jnp.float32).astype(jnp.bfloat16)
            both = lax.dot_general(spread_rows, pick, (((1,), (1,)), ((), ())), preferred_element_type=jnp.float32)
            mix[q] = jnp.where(same, both, 0.0).astype(jnp.bfloat16)

    acc[...] = jnp.zeros(acc.shape, jnp.float32) if first else acc_in[b]
    own_size = sizes[base + b]
    for q in range(states):
        a = join[base + b, q]
        place = jnp.int32(-1)
        for at, (hop, slot, _, _) in enumerate(listed):
            place = jnp.where(a - base == slot - hop * slots, at, place)

        @pl.when((a >= 0) & (place >= 0))
        def _():
            x = lax.broadcasted_iota(jnp.int32, (tile, tile), 0)
            u = lax.broadcasted_iota(jnp.int32, (tile, tile), 1)
            keep = (x < sizes[jnp.maximum(a, 0)]) & (u < own_size)
            g32 = jnp.where(keep, site_ref[0, 0, q].astype(jnp.float32), 0.0)
            gt = g32.T.astype(jnp.bfloat16)
            gy = jnp.concatenate([g32, jnp.zeros((tile, LANES - tile), jnp.float32)], axis=1)
            gy = jnp.concatenate([gy, jnp.zeros((LANES - tile, LANES), jnp.float32)], axis=0).astype(jnp.bfloat16)
            for c in range(0, chans, 2):
                y = jnp.dot(gt, slab[place, :, c * LANES : (c + 2) * LANES], preferred_element_type=jnp.float32)
                yf[pl.ds(c, tile, stride=chans), :] = y[:, :LANES]
                yf[pl.ds(c + 1, tile, stride=chans), :] = y[:, LANES:]
            for g in range(0, tile // GROUP, 2):
                one, two = (slice((g + k) * span, (g + k + 1) * span) for k in range(2))
                rhs = jnp.concatenate([yf[one, :].astype(jnp.bfloat16), yf[two, :].astype(jnp.bfloat16)], axis=1)
                v = jnp.dot(mix[q], rhs, preferred_element_type=jnp.float32)
                v = jnp.concatenate([v[:, :LANES], v[:, LANES:]], axis=0).astype(jnp.bfloat16)
                vb[g * span : (g + 2) * span, :] = v
            for g in range(0, tile * chans, CHUNK):
                some = slice(g, g + CHUNK)
                acc[some, :] += jnp.dot(vb[some, :], gy, preferred_element_type=jnp.float32)

    if last:
        for w in range(chans):
            done = acc[pl.ds(w, tile, stride=chans), :].astype(jnp.bfloat16)
            result[0, :, w * tile : (w + 1) * tile] = done[:, :tile]


def stage(owner, join, sizes, wanted, blocks, pools, tensors, ops, acc, last):
    slots, _, states, tile, _ = tensors.shape
    wide = blocks[0].shape[-1]
    chans = wide // tile
    first = acc is None
    full = tile * chans

    def whole(a):
        return pl.BlockSpec(a.shape, lambda b, *_: (0,) * a.ndim, pipeline_mode=pl.Buffered(1))

    def one(a):
        return pl.BlockSpec((1,) + a.shape[1:], lambda b, *_: (b,) + (0,) * (a.ndim - 1))

    args = list(blocks) + list(pools) + [tensors, ops]
    specs = [whole(a) for a in blocks] + [whole(a) for a in pools] + [one(tensors), whole(ops)]
    if not first:
        args.append(acc)
        specs.append(pl.BlockSpec(memory_space=pltpu.VMEM))
    if last:
        out = jax.ShapeDtypeStruct((slots, tile, wide), jnp.bfloat16)
    else:
        out = pltpu.VMEM((slots, full, LANES), jnp.float32)
    scratch = [
        pltpu.VMEM((sum(len(part) for _, part in wanted), tile, chans * LANES), jnp.bfloat16),
        pltpu.VMEM((states, GROUP * chans, GROUP * chans), jnp.bfloat16),
        pltpu.VMEM((full, LANES), jnp.float32),
        pltpu.VMEM((full, LANES), jnp.bfloat16),
    ]
    if last:
        scratch.append(pltpu.VMEM((full, LANES), jnp.float32))
    aliases = {} if first or last else {len(args) + 2: 0}
    return pl.pallas_call(
        functools.partial(stage_kernel, first, last, tuple(wanted), len(pools), slots),
        out_shape=out,
        grid_spec=pltpu.PrefetchScalarGridSpec(
            num_scalar_prefetch=3, grid=(slots,), in_specs=specs, out_specs=one(out) if last else pl.BlockSpec(memory_space=pltpu.VMEM), scratch_shapes=scratch
        ),
        input_output_aliases=aliases,
        compiler_params=pltpu.CompilerParams(vmem_limit_bytes=32 * 1024 * 1024),
        cost_estimate=pl.CostEstimate(flops=10**10, bytes_accessed=2**20, transcendentals=0),
    )(owner, join, sizes, *args)


def per_device(environment, site_tensors, operator_blocks, join_in, block_sizes):
    slots, tile, _ = environment.shape
    chans = operator_blocks.shape[0]
    owner = (lax.axis_index("region") % OWN).astype(jnp.int32)
    low = tile * 2 // 3
    own_sizes = lax.dynamic_slice_in_dim(block_sizes, owner * slots, slots, 0)
    total = jnp.sum(more_units(own_sizes, low, tile))
    ops = jnp.transpose(operator_blocks, (1, 2, 0))
    owner = owner[None]

    parts = [range(max(0, stop - 2), stop) for stop in range(slots, 1, -2)] + [range(0, 1)]
    bases, pool = pooled(owner, block_sizes, environment, parts, low)
    pool = pool_shifted(total, pool)
    here, one, two = [], [], []
    for i in range(len(parts)):
        here.append(shifted(tied(bases[i], here[i - 1] if i else pool), "region", OWN))
    pool_one = to_next(pool, "region")
    kept = pool.shape[0] // slots * (slots - 1)
    pool_two = to_second(pool[:kept], pool_one[:kept], "region")
    pools = [pool, pool_one, pool_two]
    for i in range(len(parts)):
        one.append(to_next(here[i], "region"))
        if i + 1 < len(parts):
            two.append(to_second(here[i], one[i], "region"))

    late = len(parts) - 2
    early = [(hop, i) for i in range(late) for hop in range(3)] + [(0, late)]
    rest = [(1, late), (2, late), (0, late + 1), (1, late + 1)]
    acc = None
    for chosen in (early, rest):
        blocks = [(here, one, two)[hop][i] for hop, i in chosen]
        wanted = [(hop, parts[i]) for hop, i in chosen]
        acc = stage(owner, join_in, block_sizes, wanted, blocks, pools, site_tensors, ops, acc, chosen is rest)
    return acc


def solution(mesh):
    placed = (
        P(("groups", "region"), None, None),
        P(("groups", "region"), None, None, None, None),
        P(),
        P("groups", None),
        P("groups"),
    )
    return jax.shard_map(
        per_device,
        mesh=mesh,
        in_specs=placed,
        out_specs=P(("groups", "region"), None, None),
        check_vma=False,
    )
```

```python
import functools

import jax
import jax.numpy as jnp
from jax import lax
from jax.experimental import pallas as pl
from jax.experimental.pallas import tpu as pltpu
from jax.sharding import PartitionSpec as P

OWN = 8
LANES = 128
CHUNK = 544
STEP = 16
GROUP = 4


def shifted(value, axis, steps):
    count = lax.axis_size(axis)
    return lax.ppermute(value, axis, [(source, (source + steps) % count) for source in range(count)])


def to_next(value, axis):
    count = lax.axis_size(axis)
    pairs = [(source, source + 1) for source in range(count) if source % OWN < OWN - 1]
    return lax.ppermute(value, axis, pairs)


def to_second(value, from_last, axis):
    count = lax.axis_size(axis)
    middle = OWN // 2
    regions = range(0, count, OWN)
    relay = lax.ppermute(value, axis, [(r + middle - 2, r) for r in regions])
    steps = [(0, middle)] + [(o, o + 1) for o in range(1, OWN - 1) if o != middle - 1]
    sent = jnp.where(lax.axis_index(axis) % OWN == 0, relay, from_last)
    return lax.ppermute(sent, axis, [(r + a, r + b) for r in regions for a, b in steps])


def tied(value, *after):
    return lax.optimization_barrier((value, after))[0]


def more_units(size, low, tile):
    units = (size > low).astype(jnp.int32)
    for start in range(low + STEP, tile, STEP):
        units += (size > start).astype(jnp.int32)
    return units


def base_copies(parts, low, env_ref, base_refs, sems):
    copies = []
    for number, (part, ref) in enumerate(zip(parts, base_refs)):
        source = env_ref.at[part.start : part.stop, :low]
        copies.append(pltpu.make_async_copy(source, ref, sems.at[number]))
    for copy in copies:
        copy.start()
    return copies


def pool_kernel(slots, parts, low, tile, owner, sizes, env_ref, *refs):
    *base_refs, out_ref, sems = refs
    copies = base_copies(parts, low, env_ref, base_refs, sems)
    at = jnp.int32(0)
    for slot in reversed(range(slots)):
        units = more_units(sizes[owner[0] * slots + slot], low, tile)
        for unit in range((tile - low) // STEP):

            @pl.when(unit < units)
            def _():
                out_ref[at + unit] = env_ref[slot, low + unit * STEP : low + (unit + 1) * STEP, :]

        at += units
    for copy in copies:
        copy.wait()


def pooled(owner, sizes, environment, parts, low):
    slots, tile, wide = environment.shape
    rest = tile - low
    outs = [jax.ShapeDtypeStruct((len(part), low, wide), environment.dtype) for part in parts]
    pool = jax.ShapeDtypeStruct((slots * rest // STEP, STEP, wide), environment.dtype)
    *bases, pool = pl.pallas_call(
        functools.partial(pool_kernel, slots, parts, low, tile),
        out_shape=outs + [pool],
        grid_spec=pltpu.PrefetchScalarGridSpec(
            num_scalar_prefetch=2,
            grid=(1,),
            in_specs=[pl.BlockSpec((slots, tile, wide), lambda i, *_: (0, 0, 0), pipeline_mode=pl.Buffered(1))],
            out_specs=[pl.BlockSpec(memory_space=pl.ANY)] * len(parts)
            + [pl.BlockSpec(pool.shape, lambda i, *_: (0, 0, 0))],
            scratch_shapes=[pltpu.SemaphoreType.DMA((len(parts),))],
        ),
        compiler_params=pltpu.CompilerParams(vmem_limit_bytes=60 * 1024 * 1024),
        cost_estimate=pl.CostEstimate(flops=1000, bytes_accessed=1024, transcendentals=0),
    )(owner, sizes, environment)
    return bases, pool


def pool_shifted(total, pool):
    def branch(units):
        def run(value):
            if units == 0:
                return value
            if units == value.shape[0]:
                return shifted(value, "region", OWN)
            return lax.dynamic_update_slice(value, shifted(value[:units], "region", OWN), (0, 0, 0))

        return run

    return lax.switch(total, [branch(units) for units in range(pool.shape[0] + 1)], pool)


def stage_kernel(first, last, wanted, hops, slots, owner, join, sizes, *refs):
    count = len(wanted)
    listed = [(hop, part[i], ref, i) for ref, (hop, part) in enumerate(wanted) for i in range(len(part))]
    block_refs, refs = refs[:count], refs[count:]
    pool_refs, refs = refs[:hops], refs[hops:]
    count = 0
    site_ref, ops_ref = refs[count : count + 2]
    acc_in = None if first else refs[count + 2]
    result, slab, mix, yf, vb, *rest = refs[count + 2 + (not first) :]
    tile = site_ref.shape[-1]
    states = ops_ref.shape[0]
    chans = block_refs[0].shape[-1] // tile
    span = GROUP * chans
    b = pl.program_id(0)
    base = owner[0] * slots
    acc = rest[0] if last else result.at[b]

    @pl.when(b == 0)
    def _():
        low = block_refs[0].shape[1]

        def spread(place, rows, value):
            pad = jnp.zeros((rows.stop - rows.start, LANES - tile), jnp.bfloat16)
            for w in range(chans):
                piece = value[:, w * tile : (w + 1) * tile]
                slab[place, rows, w * LANES : (w + 1) * LANES] = jnp.concatenate([piece, pad], axis=1)

        for place, (hop, slot, ref, index) in enumerate(listed):
            spread(place, slice(0, low), block_refs[ref][index])
            holder = jnp.maximum(owner[0] - hop, 0) * slots
            at = jnp.int32(0)
            for other in range(slot + 1, slots):
                at += more_units(sizes[holder + other], low, tile)
            units = more_units(sizes[holder + slot], low, tile)
            for unit in range((tile - low) // STEP):
                rows = slice(low + unit * STEP, low + (unit + 1) * STEP)

                @pl.when(unit < units)
                def _():
                    spread(place, rows, pool_refs[hop][at + unit])

                @pl.when(unit >= units)
                def _():
                    slab[place, rows, :] = jnp.zeros((STEP, chans * LANES), jnp.bfloat16)

        row = lax.broadcasted_iota(jnp.int32, (span, chans), 0)
        channel = lax.broadcasted_iota(jnp.int32, (span, chans), 1)
        pick = jnp.zeros((span, chans), jnp.bfloat16)
        for g in range(GROUP):
            pick += (row == channel + g * chans).astype(jnp.float32).astype(jnp.bfloat16)
        left = lax.broadcasted_iota(jnp.int32, (span, span), 0)
        right = lax.broadcasted_iota(jnp.int32, (span, span), 1)
        same = jnp.zeros((span, span), jnp.bool_)
        for g in range(GROUP):
            low_end, high_end = g * chans, (g + 1) * chans
            same |= (left >= low_end) & (left < high_end) & (right >= low_end) & (right < high_end)
        for q in range(states):
            spread_rows = jnp.dot(pick, ops_ref[q], preferred_element_type=jnp.float32).astype(jnp.bfloat16)
            both = lax.dot_general(spread_rows, pick, (((1,), (1,)), ((), ())), preferred_element_type=jnp.float32)
            mix[q] = jnp.where(same, both, 0.0).astype(jnp.bfloat16)

    own_size = sizes[base + b]
    for q in range(states):
        a = join[base + b, q]
        place = jnp.int32(-1)
        for at, (hop, slot, _, _) in enumerate(listed):
            place = jnp.where(a - base == slot - hop * slots, at, place)

        if q == 0:

            @pl.when((a < 0) | (place < 0))
            def _():
                acc[...] = jnp.zeros(acc.shape, jnp.float32) if first else acc_in[b]

        @pl.when((a >= 0) & (place >= 0))
        def _():
            x = lax.broadcasted_iota(jnp.int32, (tile, tile), 0)
            u = lax.broadcasted_iota(jnp.int32, (tile, tile), 1)
            keep = (x < sizes[jnp.maximum(a, 0)]) & (u < own_size)
            g32 = jnp.where(keep, site_ref[0, 0, q].astype(jnp.float32), 0.0)
            gt = g32.T.astype(jnp.bfloat16)
            gy = jnp.concatenate([g32, jnp.zeros((tile, LANES - tile), jnp.float32)], axis=1)
            gy = jnp.concatenate([gy, jnp.zeros((LANES - tile, LANES), jnp.float32)], axis=0).astype(jnp.bfloat16)
            for c in range(0, chans, 2):
                y = jnp.dot(gt, slab[place, :, c * LANES : (c + 2) * LANES], preferred_element_type=jnp.float32)
                yf[pl.ds(c, tile, stride=chans), :] = y[:, :LANES]
                yf[pl.ds(c + 1, tile, stride=chans), :] = y[:, LANES:]
            for g in range(0, tile // GROUP, 2):
                one, two = (slice((g + k) * span, (g + k + 1) * span) for k in range(2))
                rhs = jnp.concatenate([yf[one, :].astype(jnp.bfloat16), yf[two, :].astype(jnp.bfloat16)], axis=1)
                v = jnp.dot(mix[q], rhs, preferred_element_type=jnp.float32)
                v = jnp.concatenate([v[:, :LANES], v[:, LANES:]], axis=0).astype(jnp.bfloat16)
                vb[g * span : (g + 2) * span, :] = v
            for g in range(0, tile * chans, CHUNK):
                some = slice(g, g + CHUNK)
                total = jnp.dot(vb[some, :], gy, preferred_element_type=jnp.float32)
                if q:
                    total += acc[some, :]
                elif not first:
                    total += acc_in[b, some, :]
                acc[some, :] = total

    if last:
        for w in range(chans):
            done = acc[pl.ds(w, tile, stride=chans), :].astype(jnp.bfloat16)
            result[0, :, w * tile : (w + 1) * tile] = done[:, :tile]


def stage(owner, join, sizes, wanted, blocks, pools, tensors, ops, acc, last):
    slots, _, states, tile, _ = tensors.shape
    wide = blocks[0].shape[-1]
    chans = wide // tile
    first = acc is None
    full = tile * chans

    def whole(a):
        return pl.BlockSpec(a.shape, lambda b, *_: (0,) * a.ndim, pipeline_mode=pl.Buffered(1))

    def one(a):
        return pl.BlockSpec((1,) + a.shape[1:], lambda b, *_: (b,) + (0,) * (a.ndim - 1))

    args = list(blocks) + list(pools) + [tensors, ops]
    specs = [whole(a) for a in blocks] + [whole(a) for a in pools] + [one(tensors), whole(ops)]
    if not first:
        args.append(acc)
        specs.append(pl.BlockSpec(memory_space=pltpu.VMEM))
    if last:
        out = jax.ShapeDtypeStruct((slots, tile, wide), jnp.bfloat16)
    else:
        out = pltpu.VMEM((slots, full, LANES), jnp.float32)
    scratch = [
        pltpu.VMEM((sum(len(part) for _, part in wanted), tile, chans * LANES), jnp.bfloat16),
        pltpu.VMEM((states, GROUP * chans, GROUP * chans), jnp.bfloat16),
        pltpu.VMEM((full, LANES), jnp.float32),
        pltpu.VMEM((full, LANES), jnp.bfloat16),
    ]
    if last:
        scratch.append(pltpu.VMEM((full, LANES), jnp.float32))
    aliases = {} if first or last else {len(args) + 2: 0}
    return pl.pallas_call(
        functools.partial(stage_kernel, first, last, tuple(wanted), len(pools), slots),
        out_shape=out,
        grid_spec=pltpu.PrefetchScalarGridSpec(
            num_scalar_prefetch=3, grid=(slots,), in_specs=specs, out_specs=one(out) if last else pl.BlockSpec(memory_space=pltpu.VMEM), scratch_shapes=scratch
        ),
        input_output_aliases=aliases,
        compiler_params=pltpu.CompilerParams(vmem_limit_bytes=32 * 1024 * 1024),
        cost_estimate=pl.CostEstimate(flops=10**10, bytes_accessed=2**20, transcendentals=0),
    )(owner, join, sizes, *args)


def per_device(environment, site_tensors, operator_blocks, join_in, block_sizes):
    slots, tile, _ = environment.shape
    chans = operator_blocks.shape[0]
    owner = (lax.axis_index("region") % OWN).astype(jnp.int32)
    low = tile * 2 // 3
    own_sizes = lax.dynamic_slice_in_dim(block_sizes, owner * slots, slots, 0)
    total = jnp.sum(more_units(own_sizes, low, tile))
    ops = jnp.transpose(operator_blocks, (1, 2, 0))
    owner = owner[None]

    parts = [range(max(0, stop - 2), stop) for stop in range(slots, 1, -2)] + [range(0, 1)]
    bases, pool = pooled(owner, block_sizes, environment, parts, low)
    pool = pool_shifted(total, pool)
    here, one, two = [], [], []
    for i in range(len(parts)):
        here.append(shifted(tied(bases[i], here[i - 1] if i else pool), "region", OWN))
    pool_one = to_next(pool, "region")
    kept = pool.shape[0] // slots * (slots - 1)
    pool_two = to_second(pool[:kept], pool_one[:kept], "region")
    pools = [pool, pool_one, pool_two]
    for i in range(len(parts)):
        one.append(to_next(here[i], "region"))
        if i + 1 < len(parts):
            two.append(to_second(here[i], one[i], "region"))

    late = len(parts) - 2
    early = [(hop, i) for i in range(late) for hop in range(3)] + [(0, late)]
    rest = [(1, late), (2, late), (0, late + 1), (1, late + 1)]
    acc = None
    for chosen in (early, rest):
        blocks = [(here, one, two)[hop][i] for hop, i in chosen]
        wanted = [(hop, parts[i]) for hop, i in chosen]
        acc = stage(owner, join_in, block_sizes, wanted, blocks, pools, site_tensors, ops, acc, chosen is rest)
    return acc


def solution(mesh):
    placed = (
        P(("groups", "region"), None, None),
        P(("groups", "region"), None, None, None, None),
        P(),
        P("groups", None),
        P("groups"),
    )
    return jax.shard_map(
        per_device,
        mesh=mesh,
        in_specs=placed,
        out_specs=P(("groups", "region"), None, None),
        check_vma=False,
    )
```
